1024 devices in a mesh: col: 16 (over z), node: 64 (over y, x, core).
Axes of the slice: x: 4, y: 8, z: 16, core: 2. Of those that a mesh axis runs over, the one named last changes fastest.
Arguments:
- features: bfloat16 [65536, 4096], P('node', 'col'), may hold values from -6 to 6
- seed_ids: int32 [16384], P('node'), may hold values from 0 to 1023
- send_rows: int32 [64, 64, 16], P('node'), may hold values from 0 to 1023
- send_counts: int32 [64, 64], P('node'), may hold values from 1 to 16, as said below
- tile_src: int32 [128, 16], P('node'), may hold values from 0 to 15
- tile_weights: bfloat16 [128, 16, 128, 128], P('node'), may hold values from -0.125 to 0.125
- w_self: bfloat16 [4096, 1024], P('col'), may hold values from -0.0625 to 0.0625
- w_neigh: bfloat16 [4096, 1024], P('col'), may hold values from -0.0625 to 0.0625
- cotangent: bfloat16 [16384, 1024], P('node'), may hold values from -0.059814453 to 0.059814453
Outputs:
- hidden: bfloat16 [16384, 1024], P('node', 'col')
- grad_self: float32 [4096, 1024], P(('col', 'node'))
- grad_neigh: float32 [4096, 1024], P(('col', 'node'))
The draws below stay inside these ranges and needn't reach their ends.
Inputs may be any that keep to these rules, and one draw needn't show every extreme that they name: `send_counts`: live slots from one shard to another; in every draw one receiving shard gets 16 from every sender.
All inputs are finite; a program needn't handle non-finite values.
Results may differ from the reference program's by a relative error of at most 0.0051.
Values may be sent and summed in bfloat16 or wider, within the bound.
A program may use at most 32 MiB of HBM per device.

```python
import jax
import jax.numpy as jnp
from jax import lax

F = 4096
H = 1024
NODE_DEV = 1024
SEED_DEV = 256
KT = 16
CAP = 16
SBLK = 2
NODES = 65536
SEEDS = 16384
N_NODE = 64


def draw_send_counts(key, part):
    key = jax.random.fold_in(key, 5)
    first, second = jax.random.split(key)
    counts = jax.random.randint(first, (N_NODE, N_NODE), 1, CAP + 1)
    target = jax.random.randint(second, (), 0, N_NODE)
    column = lax.broadcasted_iota(jnp.int32, (N_NODE, N_NODE), 1)
    return jnp.where(column == target, CAP, counts).astype(jnp.int32)


def touch_ends(array, rng, low, largest):
    dims = array.shape
    index_at = [jax.random.randint(jax.random.fold_in(rng, axis), (), 0, dims[axis]) for axis in range(len(dims))]
    array = array.at[tuple(index_at)].set(low)
    longest = dims.index(max(dims))
    index_at[longest] = (index_at[longest] + 1) % dims[longest]
    return array.at[tuple(index_at)].set(largest)


def block_levels(key, extent, cuts, least, high):
    def one(dim, blocks):
        steps = jax.random.uniform(jax.random.fold_in(jax.random.fold_in(key, 6), dim), (blocks,), jnp.float32, least / len(cuts), high / len(cuts))
        return jnp.repeat(jnp.exp(steps), extent[dim] // blocks).reshape((-1,) + (1,) * (len(extent) - dim - 1))

    factor_of = one(*cuts[0])
    for cut in cuts[1:]:
        factor_of = factor_of * one(*cut)
    return factor_of


def noise(key, extent, scale, limit, cuts=(), kind=jnp.bfloat16):
    result = jax.random.normal(key, extent, jnp.float32) * scale
    if len(cuts) > 0:
        result = block_levels(key, extent, cuts, -0.22, 0.18) * result
    return jnp.clip(result, min=-limit, max=limit).astype(kind)


def setup_inputs(seed: int = 0) -> dict:
    key_of = jax.random.split(jax.random.key(seed), 10)
    return {
        "features": noise(key_of[0], (NODES, F), 1.0, 6.0, ((0, 64), (1, 16))),
        "seed_ids": touch_ends(jax.random.randint(key_of[1], (SEEDS,), 0, NODE_DEV), jax.random.fold_in(key_of[1], 1), 0, NODE_DEV - 1).astype(jnp.int32),
        "send_rows": touch_ends(jax.random.randint(key_of[2], (N_NODE, N_NODE, CAP), 0, NODE_DEV), jax.random.fold_in(key_of[2], 1), 0, NODE_DEV - 1).astype(jnp.int32),
        "send_counts": draw_send_counts(jax.random.fold_in(key_of[9], 71), 0),
        "tile_src": touch_ends(jax.random.randint(key_of[4], (SEEDS // 128, KT), 0, NODE_DEV // 128 + CAP * N_NODE // 128), jax.random.fold_in(key_of[4], 1), 0, (NODE_DEV // 128 + CAP * N_NODE // 128) - 1).astype(jnp.int32),
        "tile_weights": noise(key_of[5], (SEEDS // 128, KT, 128, 128), (KT * 128) ** -0.5, 0.125, ((0, 64),)),
        "w_self": noise(key_of[6], (F, H), (2 * F) ** -0.5, 0.0625, ((0, 16),)),
        "w_neigh": noise(key_of[7], (F, H), (2 * F) ** -0.5, 0.0625, ((0, 16),)),
        "cotangent": noise(key_of[8], (SEEDS, H), 0.01, 0.059814453, ((0, 64),)),
    }


def silu_slope(pre):
    sig = jax.nn.sigmoid(pre)
    return sig * (1.0 + pre * (1.0 - sig))


def reference(features, seed_ids, send_rows, send_counts, tile_src, tile_weights, w_self, w_neigh, cotangent):
    shards = features.reshape(N_NODE, NODE_DEV, F)
    seed_lists = seed_ids.reshape(N_NODE, SEED_DEV)
    tile_lists = tile_src.reshape(N_NODE, SBLK, KT)
    tile_blocks = tile_weights.reshape(N_NODE, SBLK, KT, 128, 128)
    cot_rows = cotangent.reshape(N_NODE, SEED_DEV, H)
    slot_ids = jnp.arange(CAP, dtype=jnp.int32)

    def per_shard(totals, shard_index):
        own_rows = shards[shard_index]
        picked = jax.vmap(lambda one_shard, index_list: one_shard[index_list])(shards, send_rows[:, shard_index])
        live_slots = slot_ids[None, :] < send_counts[:, shard_index][:, None]
        incoming = jnp.where(live_slots[:, :, None], picked, jnp.zeros_like(picked)).reshape(N_NODE * CAP, F)
        sources = jnp.concatenate([own_rows, incoming], axis=0).reshape(-1, 128, F)
        blocks = sources[tile_lists[shard_index]]
        neighbour_sum = jnp.einsum("skij,skjc->sic", tile_blocks[shard_index].astype(jnp.float32), blocks.astype(jnp.float32))
        neighbour_mean = neighbour_sum.reshape(SEED_DEV, F).astype(jnp.bfloat16)
        self_features = own_rows[seed_lists[shard_index]]
        pre = jnp.dot(self_features, w_self, preferred_element_type=jnp.float32) + jnp.dot(neighbour_mean, w_neigh, preferred_element_type=jnp.float32)
        hidden = jax.nn.silu(pre).astype(jnp.bfloat16)
        grad_pre = (cot_rows[shard_index].astype(jnp.float32) * silu_slope(pre)).astype(jnp.bfloat16)
        grad_self = totals[0] + jnp.dot(self_features.T, grad_pre, preferred_element_type=jnp.float32)
        grad_neigh = totals[1] + jnp.dot(neighbour_mean.T, grad_pre, preferred_element_type=jnp.float32)
        return (grad_self, grad_neigh), hidden

    start = (jnp.zeros((F, H), jnp.float32), jnp.zeros((F, H), jnp.float32))
    totals, hidden = lax.scan(per_shard, start, jnp.arange(N_NODE, dtype=jnp.int32))
    return hidden.reshape(SEEDS, H), totals[0], totals[1]
```

```python
import jax
import jax.numpy as jnp
from jax import lax
from jax.experimental import pallas as pl
from jax.experimental.pallas import tpu as pltpu
from jax.sharding import PartitionSpec as P

MESH = pl.DeviceIdType.MESH
F32 = jnp.float32
BF16 = jnp.bfloat16

NZ, NY, NX, NC = 16, 8, 4, 2
NN = NY * NX * NC

PARENT = {
    8: 6, 7: 6, 5: 6, -7: -6, -5: -6, 6: 3, -6: -3,
    4: 3, 2: 3, -4: -3, -2: -3, 3: 0, -3: 0, 1: 0, -1: 0,
}
LEAVES = (8, 7, -7, 5, -5, 4, -4, 2, -2, 1, -1)
GROUPS = ((0, 1, -1, 3), (-3, 2, -2, 4), (-4, 6, -6, 5), (7, -5, -7, 8))


def slot(offset):
    return offset % NZ


def left_half(shape):
    return lax.broadcasted_iota(jnp.int32, shape, 1) < 64


def one_hot_rows(row):
    spread = jnp.broadcast_to(row.astype(F32), (128, 128)).T
    lane = lax.broadcasted_iota(jnp.int32, (128, 128), 1).astype(F32)
    parts = [
        jnp.where(spread == lane + 128.0 * j, 1.0, 0.0).astype(BF16) for j in range(8)
    ]
    return jnp.concatenate(parts, axis=1)


def kernel(
    feat, idx, seed, tsrc, tw_hbm, ws_hbm, wn_hbm, cot_hbm,
    hid, gs, gn,
    src, out, tw, ws, wn, cot, sf, nm, part, pk, pkb, rb, sb, cp, ag, xpt, stack,
    cs, cr, xs, xr, ys, yr, fin,
    lsem, a_send, a_recv, b_send, b_recv, c_send, c_recv,
    dc_send, dc_recv, dx_send, dx_recv, dy_send, dy_recv,
):
    z = lax.axis_index("col")
    node = lax.axis_index("node")
    core = node % NC
    x = (node // NC) % NX
    y = node // (NC * NX)

    def zat(offset):
        return (z + offset + NZ) % NZ

    loads = [
        pltpu.make_async_copy(a, b, lsem.at[i])
        for i, (a, b) in enumerate((
            (feat, src.at[pl.ds(0, NN)]), (ws_hbm, ws), (tw_hbm, tw), (wn_hbm, wn), (cot_hbm, cot),
        ))
    ]
    for load in loads:
        load.start()

    barrier = pltpu.get_barrier_semaphore()

    @pl.loop(1, NN)
    def _(k):
        pl.semaphore_signal(
            barrier, inc=1, device_id=(z, (node + k) % NN), device_id_type=MESH
        )

    for d in (1, -1, 2, -2, 3, -3):
        pl.semaphore_signal(barrier, inc=1, device_id=(zat(d), node), device_id_type=MESH)
    loads[0].wait()
    feats = src[pl.ds(0, NN)].reshape(1024, 256)

    def gather(yy):
        hot = one_hot_rows(idx[pl.ds(yy, 1), :])
        rows = jnp.dot(hot, feats, preferred_element_type=F32).astype(BF16)
        out[pl.ds(pl.multiple_of(yy * 8, 8), 8)] = rows.reshape(8, 16, 256)

    def send_rows(to):
        pltpu.make_async_remote_copy(
            src_ref=out.at[to], dst_ref=src.at[NN + node], send_sem=a_send, recv_sem=a_recv,
            device_id=(z, to), device_id_type=MESH,
        ).start()

    for step, d in enumerate((4, 3, 5, 2, 6, 1, 7)):
        yy = (y + d) % NY
        gather(yy)
        if step == 0:
            pl.semaphore_wait(barrier, NN - 1 + 6)
        for j in range(8):
            send_rows(yy * 8 + j)
    gather(y)
    for j in range(1, 8):
        send_rows(y * 8 + (node + j) % 8)
    own = pltpu.make_async_copy(out.at[node], src.at[NN + node], lsem.at[5])
    own.start()

    for b in range(2):
        hot = one_hot_rows(seed[pl.ds(b, 1), :])
        sf[pl.ds(b * 128, 128), :] = jnp.dot(hot, feats, preferred_element_type=F32).astype(BF16)
    loads[1].wait()
    part[...] = jnp.dot(sf[...], ws[...], preferred_element_type=F32)

    r = lax.broadcasted_iota(jnp.int32, (512, 512), 0)
    c = lax.broadcasted_iota(jnp.int32, (512, 512), 1)
    tensor = (r >> 2) & 1
    wanted = (
        tensor * 256 + ((r >> 3) & 7) * 32 + ((r >> 6) & 3) * 8 + (r >> 8) * 4 + (r & 3)
    )
    perm = jnp.where(c == wanted, 1.0, 0.0).astype(BF16)
    stack[...] = perm
    nt = (((1,), (1,)), ((), ()))

    loads[4].wait()
    pair = pl.ds(pl.multiple_of((z // 2) * 128, 128), 128)
    c0 = cot[0:128, pair].astype(F32)
    c1 = cot[128:256, pair].astype(F32)
    even = z % 2 == 0
    left = left_half((128, 128))
    cp[...] = jnp.where(
        left,
        jnp.where(even, c0, pltpu.roll(c0, 64, 1)),
        jnp.where(even, pltpu.roll(c1, 64, 1), c1),
    )
    loads[2].wait()
    loads[3].wait()

    own.wait()
    pltpu.make_async_remote_copy(
        src_ref=src.at[pl.ds(0, NN - 1)], dst_ref=src.at[pl.ds(NN, NN - 1)],
        send_sem=a_send, recv_sem=a_recv, device_id=(z, node), device_id_type=MESH,
    ).wait_recv()
    for b in range(2):
        total = jnp.zeros((128, 256), F32)
        for k in range(0, 16, 2):
            weight = jnp.concatenate([tw[b, k], tw[b, k + 1]], axis=1)
            block = jnp.concatenate(
                [src[pl.ds(tsrc[b, k + e] * 8, 8)].reshape(128, 256) for e in range(2)], axis=0
            )
            total += jnp.dot(weight, block, preferred_element_type=F32)
        nm[pl.ds(b * 128, 128), :] = total.astype(BF16)
    for p in range(8):
        cols = pl.ds(p * 128, 128)
        value = part[:, cols] + jnp.dot(nm[...], wn[:, cols], preferred_element_type=F32)
        p0, p1 = value[0:128], value[128:256]
        first = jnp.where(left, p0, pltpu.roll(p1, 64, 1))
        second = jnp.where(left, pltpu.roll(p0, 64, 1), p1)
        pk[2 * p] = first
        pk[2 * p + 1] = second
        pkb[2 * p] = first.astype(BF16)
        pkb[2 * p + 1] = second.astype(BF16)

    def up(o, source):
        return pltpu.make_async_remote_copy(
            src_ref=source, dst_ref=rb.at[slot(o)],
            send_sem=b_send.at[slot(o)], recv_sem=b_recv.at[slot(o)],
            device_id=(zat(PARENT[o] - o), node), device_id_type=MESH,
        )

    ups = {o: up(o, pkb.at[zat(-o)]) for o in LEAVES}
    for o in LEAVES:
        ups[o].start()

    xpt[...] = (
        lax.dot_general(stack[:, 0:256], sf[...], nt, preferred_element_type=F32)
        + lax.dot_general(stack[:, 256:512], nm[...], nt, preferred_element_type=F32)
    ).astype(BF16)

    def summed(o, children):
        value = pk[zat(-o)]
        for child in children:
            ups[child].wait_recv()
            value = value + rb[slot(child)].astype(F32)
        return value

    for o, children in ((6, (7, 5, 8)), (-6, (-7, -5)), (3, (4, 2, 6)), (-3, (-4, -2, -6))):
        sb[slot(o)] = summed(o, children).astype(BF16)
        ups[o] = up(o, sb.at[slot(o)])
        ups[o].start()
    pre = summed(0, (1, -1, 3, -3))

    s = jax.nn.sigmoid(pre)
    slope = s * (1.0 + pre * (1.0 - s))
    ag[0] = (cp[...] * slope).astype(BF16)

    def down(o):
        return pltpu.make_async_remote_copy(
            src_ref=ag.at[slot(PARENT[o])], dst_ref=ag.at[slot(o)],
            send_sem=c_send.at[slot(o)], recv_sem=c_recv.at[slot(o)],
            device_id=(zat(o - PARENT[o]), node), device_id_type=MESH,
        )

    downs = {}

    def forward(*offsets):
        for o in offsets:
            downs[o] = down(o)
            downs[o].start()

    def arrived(*offsets):
        for o in offsets:
            downs[o].wait_recv()

    forward(3, -3, 1, -1)
    value = pre * s
    hid[0:128, :] = value[:, 0:64].astype(BF16)
    hid[128:256, :] = pltpu.roll(value, 64, 1)[:, 0:64].astype(BF16)

    own_rows = pl.ds(pl.multiple_of(core * 256, 256), 256)
    other_rows = pl.ds(pl.multiple_of((1 - core) * 256, 256), 256)
    kept, copies = {}, {}

    def terms(g):
        halves = []
        for q in (0, 2):
            a = ag[slot(GROUPS[g][q])].astype(F32)
            b = ag[slot(GROUPS[g][q + 1])].astype(F32)
            halves.append(jnp.concatenate(
                [
                    jnp.where(left, a, pltpu.roll(b, 64, 1)),
                    jnp.where(left, pltpu.roll(a, 64, 1), b),
                ], axis=0,
            ).astype(BF16))
        grad = jnp.concatenate(halves, axis=1)
        cs[g] = jnp.dot(xpt[other_rows, :], grad, preferred_element_type=F32).astype(BF16)
        copies["c", g] = pltpu.make_async_remote_copy(
            src_ref=cs.at[g], dst_ref=cr.at[g], send_sem=dc_send.at[g], recv_sem=dc_recv.at[g],
            device_id=(z, node + 1 - 2 * core), device_id_type=MESH,
        )
        copies["c", g].start()
        kept[g] = jnp.dot(xpt[own_rows, :], grad, preferred_element_type=F32)

    def over_x(g):
        copies["c", g].wait_recv()
        total = kept[g] + cr[g].astype(F32)
        for xx in range(4):
            xs[g, xx] = total[xx * 64:(xx + 1) * 64]
        for xx in range(4):
            cs[g, pl.ds(xx * 64, 64)] = total[xx * 64:(xx + 1) * 64].astype(BF16)

    def start_x(g):
        copies["c", g].wait_send()
        over_x(g)
        for i in range(1, NX):
            to = (x + i) % NX
            pltpu.make_async_remote_copy(
                src_ref=cs.at[g, pl.ds(pl.multiple_of(to * 64, 64), 64)], dst_ref=xr.at[g, i - 1],
                send_sem=dx_send.at[g], recv_sem=dx_recv.at[g],
                device_id=(z, (y * NX + to) * NC + core), device_id_type=MESH,
            ).start()

    def all_x(g):
        return pltpu.make_async_remote_copy(
            src_ref=xr.at[g], dst_ref=xr.at[g], send_sem=dx_send.at[g], recv_sem=dx_recv.at[g],
            device_id=(z, node), device_id_type=MESH,
        )

    def all_y(g):
        return pltpu.make_async_remote_copy(
            src_ref=yr.at[g], dst_ref=yr.at[g], send_sem=dy_send.at[g], recv_sem=dy_recv.at[g],
            device_id=(z, node), device_id_type=MESH,
        )

    def start_y(g):
        all_x(g).wait_recv()
        total = xs[g, x]
        for i in range(NX - 1):
            total = total + xr[g, i].astype(F32)
        ys[g] = total.reshape(NY, 8, 256)
        for i in (4, 3, 5, 2, 6, 1, 7):
            to = (y + i) % NY
            pltpu.make_async_remote_copy(
                src_ref=ys.at[g, to], dst_ref=yr.at[g, i - 1],
                send_sem=dy_send.at[g], recv_sem=dy_recv.at[g],
                device_id=(z, (to * NX + x) * NC + core), device_id_type=MESH,
            ).start()

    half = lax.broadcasted_iota(jnp.int32, (8, 128), 1) // 64

    def finish(g):
        all_y(g).wait_recv()
        total = ys[g, y]
        for i in range(NY - 1):
            total = total + yr[g, i]
        for q in range(4):
            chunk = zat(-GROUPS[g][q])
            side = chunk % 2
            tile = total[:, (q // 2) * 128:(q // 2 + 1) * 128]
            tile = jnp.where(side == q % 2, tile, pltpu.roll(tile, 64, 1))
            fin[chunk // 2] = jnp.where(half == side, tile, fin[chunk // 2])

    fin[...] = jnp.zeros_like(fin)
    arrived(3)
    forward(6, 4, 2)
    arrived(-3)
    forward(-6, -4, -2)
    arrived(1, -1)
    terms(0)
    arrived(6)
    forward(8, 7, 5)
    arrived(-6)
    forward(-7, -5)
    arrived(2, -2, 4)
    terms(1)
    start_x(0)
    arrived(-4, 5)
    terms(2)
    start_x(1)
    start_y(0)
    arrived(7, -5, -7, 8)
    terms(3)
    start_x(2)
    start_y(1)
    start_x(3)
    start_y(2)
    finish(0)
    start_y(3)
    finish(1)
    finish(2)
    finish(3)
    for p in range(8):
        cols = pl.ds(p * 128, 128)
        gs[:, cols] = fin[p, 0:4, :]
        gn[:, cols] = fin[p, 4:8, :]

    pltpu.make_async_remote_copy(
        src_ref=out.at[pl.ds(0, NN - 1)], dst_ref=out.at[pl.ds(0, NN - 1)],
        send_sem=a_send, recv_sem=a_recv, device_id=(z, node), device_id_type=MESH,
    ).wait_send()
    for o in PARENT:
        ups[o].wait_send()
        downs[o].wait_send()
    for g in range(4):
        all_x(g).wait_send()
        all_y(g).wait_send()


def on_device(
    features, seed_ids, send_rows, send_counts, tile_src, tile_weights, w_self, w_neigh, cotangent
):
    slot_ids = lax.broadcasted_iota(jnp.int32, send_rows.shape[1:], 1)
    live = slot_ids < send_counts[0][:, None]
    idx = jnp.where(live, send_rows[0], -1).reshape(8, 128)
    any_space = pl.BlockSpec(memory_space=pl.ANY)
    vmem = pl.BlockSpec(memory_space=pltpu.VMEM)
    smem = pl.BlockSpec(memory_space=pltpu.SMEM)
    dma = pltpu.SemaphoreType.DMA
    return pl.pallas_call(
        kernel,
        out_shape=(
            jax.ShapeDtypeStruct((256, 64), BF16),
            jax.ShapeDtypeStruct((4, 1024), F32),
            jax.ShapeDtypeStruct((4, 1024), F32),
        ),
        in_specs=[any_space, vmem, vmem, smem, any_space, any_space, any_space, any_space],
        out_specs=(vmem, vmem, vmem),
        scratch_shapes=[
            pltpu.VMEM((2 * NN, 16, 256), BF16),
            pltpu.VMEM((NN, 16, 256), BF16),
            pltpu.VMEM((2, 16, 128, 128), BF16),
            pltpu.VMEM((256, 1024), BF16),
            pltpu.VMEM((256, 1024), BF16),
            pltpu.VMEM((256, 1024), BF16),
            pltpu.VMEM((256, 256), BF16),
            pltpu.VMEM((256, 256), BF16),
            pltpu.VMEM((256, 1024), F32),
            pltpu.VMEM((NZ, 128, 128), F32),
            pltpu.VMEM((NZ, 128, 128), BF16),
            pltpu.VMEM((NZ, 128, 128), BF16),
            pltpu.VMEM((NZ, 128, 128), BF16),
            pltpu.VMEM((128, 128), F32),
            pltpu.VMEM((NZ, 128, 128), BF16),
            pltpu.VMEM((512, 256), BF16),
            pltpu.VMEM((512, 512), BF16),
            pltpu.VMEM((4, 256, 256), BF16),
            pltpu.VMEM((4, 256, 256), BF16),
            pltpu.VMEM((4, NX, 64, 256), F32),
            pltpu.VMEM((4, NX - 1, 64, 256), BF16),
            pltpu.VMEM((4, NY, 8, 256), F32),
            pltpu.VMEM((4, NY - 1, 8, 256), F32),
            pltpu.VMEM((8, 8, 128), F32),
            dma((6,)),
            dma,
            dma,
            dma((NZ,)),
            dma((NZ,)),
            dma((NZ,)),
            dma((NZ,)),
            dma((4,)),
            dma((4,)),
            dma((4,)),
            dma((4,)),
            dma((4,)),
            dma((4,)),
        ],
        compiler_params=pltpu.CompilerParams(
            collective_id=0, has_side_effects=True, vmem_limit_bytes=40 * 1024 * 1024
        ),
        name="sage_layer",
    )(
        features.reshape(64, 16, 256), idx, seed_ids.reshape(2, 128), tile_src, tile_weights,
        w_self, w_neigh, cotangent,
    )


def solution(mesh):
    in_specs = (
        P("node", "col"),
        P("node"),
        P("node", None, None),
        P("node", None),
        P("node", None),
        P("node", None, None, None),
        P("col", None),
        P("col", None),
        P("node", None),
    )
    out_specs = (P("node", "col"), P(("col", "node"), None), P(("col", "node"), None))
    return jax.shard_map(
        on_device, mesh=mesh, in_specs=in_specs, out_specs=out_specs, check_vma=False
    )
```

```python
import jax
import jax.numpy as jnp
from jax import lax
from jax.experimental import pallas as pl
from jax.experimental.pallas import tpu as pltpu
from jax.sharding import PartitionSpec as P

MESH = pl.DeviceIdType.MESH
F32 = jnp.float32
BF16 = jnp.bfloat16

NZ, NY, NX, NC = 16, 8, 4, 2
NN = NY * NX * NC
NBAR = NN - 1 + 6

PARENT = {
    8: 6, 7: 6, 5: 6, -7: -6, -5: -6, 6: 3, -6: -3,
    4: 3, 2: 3, -4: -3, -2: -3, 3: 0, -3: 0, 1: 0, -1: 0,
}
LEAVES = (8, 7, -7, 5, -5, 4, -4, 2, -2, 1, -1)
GROUPS = ((0, 1, -1, 3), (-3, 2, -2, 4), (-4, 6, -6, 5), (7, -5, -7, 8))


def slot(offset):
    return offset % NZ


def left_half(shape):
    return lax.broadcasted_iota(jnp.int32, shape, 1) < 64


def one_hot_rows(spread):
    lane = lax.broadcasted_iota(jnp.int32, (128, 128), 1).astype(F32)
    parts = [
        jnp.where(spread == lane + 128.0 * j, 1.0, 0.0).astype(BF16) for j in range(8)
    ]
    return jnp.concatenate(parts, axis=1)


def kernel(
    feat, rows_hbm, counts_hbm, seed_hbm, tsrc_hbm, tw_hbm, ws_hbm, wn_hbm, cot_hbm,
    hid, grads,
    rows, counts, seed, tsrc, slots, src, out, tw, ws, wn, cot, sf, nm, part, pk, pkb, rb, sb, cp, ag, xpt, stack,
    cs, cr, xs, xb, xr, lx, lb, lr, ys, yb, yr, fin,
    lsem, a_send, a_recv, b_send, b_recv, c_send, c_recv,
    dc_send, dc_recv, dx_send, dx_recv, dy_send, dy_recv,
):
    z = lax.axis_index("col")
    node = lax.axis_index("node")
    core = node % NC
    x = (node // NC) % NX
    y = node // (NC * NX)

    def zat(offset):
        return (z + offset + NZ) % NZ

    loads = [
        pltpu.make_async_copy(a, b, lsem.at[i])
        for i, (a, b) in enumerate((
            (rows_hbm, rows), (counts_hbm, counts), (feat, src.at[pl.ds(0, NN)]), (seed_hbm, seed),
            (ws_hbm, ws), (cot_hbm, cot), (tsrc_hbm, tsrc), (tw_hbm, tw), (wn_hbm, wn),
        ))
    ]
    for load in loads[:3]:
        load.start()

    barrier = pltpu.get_barrier_semaphore()
    for d in (4, 3, 5, 2, 6, 1, 7, 0):
        for j in range(8):
            if d or j:
                to = ((y + d) % NY) * 8 + (node + j) % 8
                pl.semaphore_signal(barrier, inc=1, device_id=(z, to), device_id_type=MESH)
    for d in (3, -3, 2, -2, 1, -1):
        pl.semaphore_signal(barrier, inc=1, device_id=(zat(d), node), device_id_type=MESH)
    for load in loads[3:]:
        load.start()

    loads[0].wait()
    loads[1].wait()
    live = lax.broadcasted_iota(jnp.int32, (16, 64), 0) < counts[...]
    table = jnp.where(live, rows[...], -1).astype(F32)
    table = jnp.concatenate([table, jnp.zeros((16, 64), F32)], axis=1)
    slots[...] = jnp.concatenate([table, jnp.zeros((112, 128), F32)], axis=0).T
    loads[2].wait()
    feats = src[pl.ds(0, NN)].reshape(1024, 256)
    own_slot = (
        lax.broadcasted_iota(jnp.int32, (128, 128), 0) % 16
        == lax.broadcasted_iota(jnp.int32, (128, 128), 1)
    )

    def gather(yy):
        tile = slots[pl.ds(pl.multiple_of(yy * 8, 8), 8), :]
        tile = jnp.broadcast_to(tile[:, None, :], (8, 16, 128)).reshape(128, 128)
        spread = jnp.sum(jnp.where(own_slot, tile, 0.0), axis=1, keepdims=True)
        hot = one_hot_rows(spread)
        picked = jnp.dot(hot, feats, preferred_element_type=F32).astype(BF16)
        out[pl.ds(pl.multiple_of(yy * 8, 8), 8)] = picked.reshape(8, 16, 256)

    def send_rows(to):
        pltpu.make_async_remote_copy(
            src_ref=out.at[to], dst_ref=src.at[NN + node], send_sem=a_send, recv_sem=a_recv,
            device_id=(z, to), device_id_type=MESH,
        ).start()

    for step, d in enumerate((4, 3, 5, 2, 6, 1, 7)):
        yy = (y + d) % NY
        gather(yy)
        if step == 0:
            pl.semaphore_wait(barrier, NBAR)
        for j in range(8):
            send_rows(yy * 8 + (node + j) % 8)
    gather(y)
    for j in range(1, 8):
        send_rows(y * 8 + (node + j) % 8)
    own = pltpu.make_async_copy(out.at[node], src.at[NN + node], lsem.at[9])
    own.start()

    loads[3].wait()
    for b in range(2):
        hot = one_hot_rows(jnp.broadcast_to(seed[b:b + 1, :].astype(F32), (128, 128)).T)
        sf[pl.ds(b * 128, 128), :] = jnp.dot(hot, feats, preferred_element_type=F32).astype(BF16)
    loads[4].wait()
    part[...] = jnp.dot(sf[...], ws[...], preferred_element_type=F32)

    r = lax.broadcasted_iota(jnp.int32, (512, 512), 0)
    c = lax.broadcasted_iota(jnp.int32, (512, 512), 1)
    tensor = (r >> 2) & 1
    wanted = (
        tensor * 256 + ((r >> 3) & 7) * 32 + ((r >> 6) & 3) * 8 + (r >> 8) * 4 + (r & 3)
    )
    perm = jnp.where(c == wanted, 1.0, 0.0).astype(BF16)
    stack[...] = perm
    nt = (((1,), (1,)), ((), ()))

    loads[5].wait()
    pair = pl.ds(pl.multiple_of((z // 2) * 128, 128), 128)
    c0 = cot[0:128, pair].astype(F32)
    c1 = cot[128:256, pair].astype(F32)
    even = z % 2 == 0
    left = left_half((128, 128))
    cp[...] = jnp.where(
        left,
        jnp.where(even, c0, pltpu.roll(c0, 64, 1)),
        jnp.where(even, pltpu.roll(c1, 64, 1), c1),
    )
    for load in loads[6:]:
        load.wait()

    own.wait()
    pltpu.make_async_remote_copy(
        src_ref=src.at[pl.ds(0, NN - 1)], dst_ref=src.at[pl.ds(NN, NN - 1)],
        send_sem=a_send, recv_sem=a_recv, device_id=(z, node), device_id_type=MESH,
    ).wait_recv()
    for b in range(2):
        total = jnp.zeros((128, 256), F32)
        for k in range(0, 16, 2):
            weight = jnp.concatenate([tw[b, k], tw[b, k + 1]], axis=1)
            block = jnp.concatenate(
                [src[pl.ds(tsrc[b, k + e] * 8, 8)].reshape(128, 256) for e in range(2)], axis=0
            )
            total += jnp.dot(weight, block, preferred_element_type=F32)
        nm[pl.ds(b * 128, 128), :] = total.astype(BF16)

    def up(o, source):
        return pltpu.make_async_remote_copy(
            src_ref=source, dst_ref=rb.at[slot(o)],
            send_sem=b_send.at[slot(o)], recv_sem=b_recv.at[slot(o)],
            device_id=(zat(PARENT[o] - o), node), device_id_type=MESH,
        )

    ups = {o: up(o, pkb.at[zat(-o)]) for o in LEAVES}
    for pairs, leaves in (((4, 3, -3), (8, 7, -7)), ((2, -2), (5, -5, 4, -4)), ((1, -1, 0), (2, -2, 1, -1))):
        for q in pairs:
            p = (z // 2 + q + 8) % 8
            cols = pl.ds(pl.multiple_of(p * 128, 128), 128)
            value = part[:, cols] + jnp.dot(nm[...], wn[:, cols], preferred_element_type=F32)
            p0, p1 = value[0:128], value[128:256]
            first = jnp.where(left, p0, pltpu.roll(p1, 64, 1))
            second = jnp.where(left, pltpu.roll(p0, 64, 1), p1)
            pk[2 * p] = first
            pk[2 * p + 1] = second
            pkb[2 * p] = first.astype(BF16)
            pkb[2 * p + 1] = second.astype(BF16)
        for o in leaves:
            ups[o].start()

    xpt[...] = (
        lax.dot_general(stack[:, 0:256], sf[...], nt, preferred_element_type=F32)
        + lax.dot_general(stack[:, 256:512], nm[...], nt, preferred_element_type=F32)
    ).astype(BF16)

    def summed(o, children):
        value = pk[zat(-o)]
        for child in children:
            ups[child].wait_recv()
            value = value + rb[slot(child)].astype(F32)
        return value

    for o, children in ((6, (7, 5, 8)), (-6, (-7, -5)), (3, (4, 2, 6)), (-3, (-4, -2, -6))):
        sb[slot(o)] = summed(o, children).astype(BF16)
        ups[o] = up(o, sb.at[slot(o)])
        ups[o].start()
    pre = summed(0, (1, -1, 3, -3))

    s = jax.nn.sigmoid(pre)
    slope = s * (1.0 + pre * (1.0 - s))
    ag[0] = (cp[...] * slope).astype(BF16)

    def down(o):
        return pltpu.make_async_remote_copy(
            src_ref=ag.at[slot(PARENT[o])], dst_ref=ag.at[slot(o)],
            send_sem=c_send.at[slot(o)], recv_sem=c_recv.at[slot(o)],
            device_id=(zat(o - PARENT[o]), node), device_id_type=MESH,
        )

    downs = {}

    def forward(*offsets):
        for o in offsets:
            downs[o] = down(o)
            downs[o].start()

    def arrived(*offsets):
        for o in offsets:
            downs[o].wait_recv()

    forward(3, -3, 1, -1)
    value = pre * s
    value = value.T
    hid[:, 0:128] = value[0:64].astype(BF16)
    hid[:, 128:256] = value[64:128].astype(BF16)

    own_rows = pl.ds(pl.multiple_of(core * 256, 256), 256)
    other_rows = pl.ds(pl.multiple_of((1 - core) * 256, 256), 256)
    kept, copies = {}, {}

    def gathered(g):
        halves = []
        for q in (0, 2):
            a = ag[slot(GROUPS[g][q])].astype(F32)
            b = ag[slot(GROUPS[g][q + 1])].astype(F32)
            halves.append(jnp.concatenate(
                [
                    jnp.where(left, a, pltpu.roll(b, 64, 1)),
                    jnp.where(left, pltpu.roll(a, 64, 1), b),
                ], axis=0,
            ).astype(BF16))
        return jnp.concatenate(halves, axis=1)

    def terms(g):
        grad = gathered(g)
        cs[g] = jnp.dot(xpt[other_rows, :], grad, preferred_element_type=F32).astype(BF16)
        copies[g] = pltpu.make_async_remote_copy(
            src_ref=cs.at[g], dst_ref=cr.at[g], send_sem=dc_send.at[g], recv_sem=dc_recv.at[g],
            device_id=(z, node + 1 - 2 * core), device_id_type=MESH,
        )
        copies[g].start()
        kept[g] = jnp.dot(xpt[own_rows, :], grad, preferred_element_type=F32)

    def start_x(g):
        copies[g].wait_recv()
        total = kept[g] + cr[g].astype(F32)
        xs[g] = total
        xb[g] = total.astype(BF16)
        for i in (2, 1, 3):
            to = (x + i) % NX
            pltpu.make_async_remote_copy(
                src_ref=xb.at[g, pl.ds(pl.multiple_of(to * 64, 64), 64)], dst_ref=xr.at[g, i - 1],
                send_sem=dx_send.at[g], recv_sem=dx_recv.at[g],
                device_id=(z, (y * NX + to) * NC + core), device_id_type=MESH,
            ).start()

    last = len(GROUPS) - 1

    def last_terms():
        total = jnp.dot(xpt[...], gathered(last), preferred_element_type=F32)
        lb[...] = total.astype(BF16)
        for i in (4, 5, 3, 2, 6, 1, 7):
            to = (node + i) % 8
            rows_to = (to % NC) * 256 + (to // NC) * 64
            pltpu.make_async_remote_copy(
                src_ref=lb.at[pl.ds(pl.multiple_of(rows_to, 64), 64)], dst_ref=lr.at[i - 1],
                send_sem=dx_send.at[last], recv_sem=dx_recv.at[last],
                device_id=(z, y * 8 + to), device_id_type=MESH,
            ).start()
        lx[...] = total

    def all_x(g):
        ref = lr if g == last else xr.at[g]
        return pltpu.make_async_remote_copy(
            src_ref=ref, dst_ref=ref, send_sem=dx_send.at[g], recv_sem=dx_recv.at[g],
            device_id=(z, node), device_id_type=MESH,
        )

    def all_y(g):
        return pltpu.make_async_remote_copy(
            src_ref=yr.at[g], dst_ref=yr.at[g], send_sem=dy_send.at[g], recv_sem=dy_recv.at[g],
            device_id=(z, node), device_id_type=MESH,
        )

    def start_y(g):
        all_x(g).wait_recv()
        if g == last:
            total = lx[pl.ds(pl.multiple_of(core * 256 + x * 64, 64), 64), :]
            for i in range(7):
                total = total + lr[i].astype(F32)
        else:
            total = xs[g, pl.ds(pl.multiple_of(x * 64, 64), 64), :]
            for i in range(NX - 1):
                total = total + xr[g, i].astype(F32)
        total = total.reshape(NY, 8, 256)
        total = jnp.concatenate([total[:, :, 0:128], total[:, :, 128:256]], axis=1)
        ys[g] = total
        yb[g] = total.astype(BF16)
        for i in (4, 3, 5, 2, 6, 1, 7):
            to = (y + i) % NY
            pltpu.make_async_remote_copy(
                src_ref=yb.at[g, to], dst_ref=yr.at[g, i - 1],
                send_sem=dy_send.at[g], recv_sem=dy_recv.at[g],
                device_id=(z, (to * NX + x) * NC + core), device_id_type=MESH,
            ).start()

    half = lax.broadcasted_iota(jnp.int32, (8, 128), 1) // 64

    def finish(g):
        all_y(g).wait_recv()
        total = ys[g, y]
        for i in range(NY - 1):
            total = total + yr[g, i].astype(F32)
        for q in range(4):
            chunk = zat(-GROUPS[g][q])
            side = chunk % 2
            tile = total[(q // 2) * 8:(q // 2 + 1) * 8]
            tile = jnp.where(side == q % 2, tile, pltpu.roll(tile, 64, 1))
            fin[chunk // 2] = jnp.where(half == side, tile, fin[chunk // 2])

    fin[...] = jnp.zeros_like(fin)
    arrived(3)
    forward(6, 4, 2)
    arrived(-3)
    forward(-6, -4, -2)
    arrived(1, -1)
    terms(0)
    arrived(6)
    forward(8, 7, 5)
    arrived(-6)
    forward(-7, -5)
    arrived(2, -2, 4)
    terms(1)
    start_x(0)
    arrived(-4, 5)
    terms(2)
    start_x(1)
    start_y(0)
    arrived(7, -5, -7, 8)
    last_terms()
    start_x(2)
    start_y(1)
    start_y(2)
    finish(0)
    start_y(3)
    finish(1)
    finish(2)
    finish(3)
    for p in range(8):
        cols = pl.ds(p * 128, 128)
        grads[:, cols] = fin[p]

    pltpu.make_async_remote_copy(
        src_ref=out.at[pl.ds(0, NN - 1)], dst_ref=out.at[pl.ds(0, NN - 1)],
        send_sem=a_send, recv_sem=a_recv, device_id=(z, node), device_id_type=MESH,
    ).wait_send()
    for o in PARENT:
        ups[o].wait_send()
        downs[o].wait_send()
    for g in range(4):
        if g != last:
            copies[g].wait_send()
        all_x(g).wait_send()
        all_y(g).wait_send()


def write_out(hidden, grads, hid, grad_self, grad_neigh, sems):
    copies = [
        pltpu.make_async_copy(hidden, hid, sems.at[0]),
        pltpu.make_async_copy(grads.at[0:4], grad_self, sems.at[1]),
        pltpu.make_async_copy(grads.at[4:8], grad_neigh, sems.at[2]),
    ]
    for copy in copies:
        copy.start()
    for copy in copies:
        copy.wait()


def on_device(
    features, seed_ids, send_rows, send_counts, tile_src, tile_weights, w_self, w_neigh, cotangent
):
    hbm = pl.BlockSpec(memory_space=pltpu.HBM)
    vmem = pl.BlockSpec(memory_space=pltpu.VMEM)
    dma = pltpu.SemaphoreType.DMA
    hidden_t, grads = pl.pallas_call(
        kernel,
        out_shape=(
            jax.ShapeDtypeStruct((64, 256), BF16),
            jax.ShapeDtypeStruct((8, 1024), F32),
        ),
        in_specs=[hbm] * 9,
        out_specs=(vmem, vmem),
        scratch_shapes=[
            pltpu.VMEM((16, 64), jnp.int32),
            pltpu.VMEM((1, 64), jnp.int32),
            pltpu.VMEM((2, 128), jnp.int32),
            pltpu.SMEM((2, 16), jnp.int32),
            pltpu.VMEM((128, 128), F32),
            pltpu.VMEM((2 * NN, 16, 256), BF16),
            pltpu.VMEM((NN, 16, 256), BF16),
            pltpu.VMEM((2, 16, 128, 128), BF16),
            pltpu.VMEM((256, 1024), BF16),
            pltpu.VMEM((256, 1024), BF16),
            pltpu.VMEM((256, 1024), BF16),
            pltpu.VMEM((256, 256), BF16),
            pltpu.VMEM((256, 256), BF16),
            pltpu.VMEM((256, 1024), F32),
            pltpu.VMEM((NZ, 128, 128), F32),
            pltpu.VMEM((NZ, 128, 128), BF16),
            pltpu.VMEM((NZ, 128, 128), BF16),
            pltpu.VMEM((NZ, 128, 128), BF16),
            pltpu.VMEM((128, 128), F32),
            pltpu.VMEM((NZ, 128, 128), BF16),
            pltpu.VMEM((512, 256), BF16),
            pltpu.VMEM((512, 512), BF16),
            pltpu.VMEM((3, 256, 256), BF16),
            pltpu.VMEM((3, 256, 256), BF16),
            pltpu.VMEM((3, 256, 256), F32),
            pltpu.VMEM((3, 256, 256), BF16),
            pltpu.VMEM((3, NX - 1, 64, 256), BF16),
            pltpu.VMEM((512, 256), F32),
            pltpu.VMEM((512, 256), BF16),
            pltpu.VMEM((7, 64, 256), BF16),
            pltpu.VMEM((4, NY, 16, 128), F32),
            pltpu.VMEM((4, NY, 16, 128), BF16),
            pltpu.VMEM((4, NY - 1, 16, 128), BF16),
            pltpu.VMEM((8, 8, 128), F32),
            dma((10,)),
            dma,
            dma,
            dma((NZ,)),
            dma((NZ,)),
            dma((NZ,)),
            dma((NZ,)),
            dma((3,)),
            dma((3,)),
            dma((4,)),
            dma((4,)),
            dma((4,)),
            dma((4,)),
        ],
        compiler_params=pltpu.CompilerParams(
            collective_id=0, has_side_effects=True, vmem_limit_bytes=60 * 1024 * 1024
        ),
        name="sage_layer",
    )(
        features.reshape(64, 16, 256), send_rows[0].T, send_counts, seed_ids.reshape(2, 128),
        tile_src, tile_weights, w_self, w_neigh, cotangent,
    )
    hidden_t, grad_self, grad_neigh = pl.pallas_call(
        write_out,
        out_shape=(
            jax.ShapeDtypeStruct((64, 256), BF16),
            jax.ShapeDtypeStruct((4, 1024), F32),
            jax.ShapeDtypeStruct((4, 1024), F32),
        ),
        in_specs=[vmem] * 2,
        out_specs=(hbm,) * 3,
        scratch_shapes=[dma((3,))],
        name="write_out",
    )(hidden_t, grads)
    return hidden_t.T, grad_self, grad_neigh


def solution(mesh):
    in_specs = (
        P("node", "col"),
        P("node"),
        P("node", None, None),
        P("node", None),
        P("node", None),
        P("node", None, None, None),
        P("col", None),
        P("col", None),
        P("node", None),
    )
    out_specs = (P("node", "col"), P(("col", "node"), None), P(("col", "node"), None))
    return jax.shard_map(
        on_device, mesh=mesh, in_specs=in_specs, out_specs=out_specs, check_vma=False
    )
```

```python
import jax
import jax.numpy as jnp
from jax import lax
from jax.experimental import pallas as pl
from jax.experimental.pallas import tpu as pltpu
from jax.sharding import PartitionSpec as P

MESH = pl.DeviceIdType.MESH
F32 = jnp.float32
BF16 = jnp.bfloat16

NZ, NY, NX, NC = 16, 8, 4, 2
NN = NY * NX * NC
NBAR = NN - 1 + 6

PARENT = {
    8: 6, -8: -6, 7: 6, 5: 6, -7: -6, -5: -6, 6: 3, -6: -3,
    4: 3, 2: 3, -4: -3, -2: -3, 3: 0, -3: 0, 1: 0, -1: 0,
}
LEAVES = (8, -8, 7, -7, 5, -5, 4, -4, 2, -2, 1, -1)
HALVES = {8: 0, -8: 64}
GROUPS = ((0, 1, -1, 3), (-3, 2, -2, 4), (-4, 6, -6, 5), (7, -5, -7, 8))


def slot(offset):
    return offset % NZ


def sem(offset):
    return 0 if offset == -8 else slot(offset)


def rows_of(ref, offset):
    return ref.at[pl.ds(HALVES[offset], 64)] if offset in HALVES else ref


def left_half(shape):
    return lax.broadcasted_iota(jnp.int32, shape, 1) < 64


def one_hot_rows(spread):
    lane = lax.broadcasted_iota(jnp.int32, (128, 128), 1).astype(F32)
    parts = [
        jnp.where(spread == lane + 128.0 * j, 1.0, 0.0).astype(BF16) for j in range(8)
    ]
    return jnp.concatenate(parts, axis=1)


def kernel(
    feat, rows_hbm, counts_hbm, seed_hbm, tsrc_hbm, tw_hbm, ws_hbm, wn_hbm, cot_hbm,
    hid, grads,
    rows, counts, seed, tsrc, slots, src, out, tw, ws, wn, cot, sf, nm, part, pk, pkb, rb, sb, cp, ag, xpt, stack,
    cs, cr, xs, xb, xr, ys, yb, yr, fin,
    lsem, a_send, a_recv, b_send, b_recv, c_send, c_recv,
    dc_send, dc_recv, dx_send, dx_recv, dy_send, dy_recv,
):
    z = lax.axis_index("col")
    node = lax.axis_index("node")
    core = node % NC
    x = (node // NC) % NX
    y = node // (NC * NX)

    def zat(offset):
        return (z + offset + NZ) % NZ

    loads = [
        pltpu.make_async_copy(a, b, lsem.at[i])
        for i, (a, b) in enumerate((
            (rows_hbm, rows), (counts_hbm, counts), (feat, src.at[pl.ds(0, NN)]), (seed_hbm, seed),
            (ws_hbm, ws), (cot_hbm, cot), (tsrc_hbm, tsrc), (tw_hbm, tw), (wn_hbm, wn),
        ))
    ]
    for load in loads[:3]:
        load.start()

    barrier = pltpu.get_barrier_semaphore()
    for d in (4, 3, 5, 2, 6, 1, 7, 0):
        for j in range(8):
            if d or j:
                to = ((y + d) % NY) * 8 + (node + j) % 8
                pl.semaphore_signal(barrier, inc=1, device_id=(z, to), device_id_type=MESH)
    for d in (3, -3, 2, -2, 1, -1):
        pl.semaphore_signal(barrier, inc=1, device_id=(zat(d), node), device_id_type=MESH)
    for load in loads[3:]:
        load.start()

    loads[0].wait()
    loads[1].wait()
    live = lax.broadcasted_iota(jnp.int32, (16, 64), 0) < counts[...]
    table = jnp.where(live, rows[...], -1).astype(F32)
    table = jnp.concatenate([table, jnp.zeros((16, 64), F32)], axis=1)
    slots[...] = jnp.concatenate([table, jnp.zeros((112, 128), F32)], axis=0).T
    loads[2].wait()
    feats = src[pl.ds(0, NN)].reshape(1024, 256)
    own_slot = (
        lax.broadcasted_iota(jnp.int32, (128, 128), 0) % 16
        == lax.broadcasted_iota(jnp.int32, (128, 128), 1)
    )

    def gather(yy):
        tile = slots[pl.ds(pl.multiple_of(yy * 8, 8), 8), :]
        tile = jnp.broadcast_to(tile[:, None, :], (8, 16, 128)).reshape(128, 128)
        spread = jnp.sum(jnp.where(own_slot, tile, 0.0), axis=1, keepdims=True)
        hot = one_hot_rows(spread)
        picked = jnp.dot(hot, feats, preferred_element_type=F32).astype(BF16)
        out[pl.ds(pl.multiple_of(yy * 8, 8), 8)] = picked.reshape(8, 16, 256)

    def send_rows(to):
        pltpu.make_async_remote_copy(
            src_ref=out.at[to], dst_ref=src.at[NN + node], send_sem=a_send, recv_sem=a_recv,
            device_id=(z, to), device_id_type=MESH,
        ).start()

    for step, d in enumerate((4, 3, 5, 2, 6, 1, 7)):
        yy = (y + d) % NY
        gather(yy)
        if step == 0:
            pl.semaphore_wait(barrier, NBAR)
        for j in range(8):
            send_rows(yy * 8 + (node + j) % 8)
    gather(y)
    for j in range(1, 8):
        send_rows(y * 8 + (node + j) % 8)
    own = pltpu.make_async_copy(out.at[node], src.at[NN + node], lsem.at[9])
    own.start()

    loads[3].wait()
    for b in range(2):
        hot = one_hot_rows(jnp.broadcast_to(seed[b:b + 1, :].astype(F32), (128, 128)).T)
        sf[pl.ds(b * 128, 128), :] = jnp.dot(hot, feats, preferred_element_type=F32).astype(BF16)
    loads[4].wait()
    part[...] = jnp.dot(sf[...], ws[...], preferred_element_type=F32)

    r = lax.broadcasted_iota(jnp.int32, (512, 512), 0)
    c = lax.broadcasted_iota(jnp.int32, (512, 512), 1)
    tensor = (r >> 2) & 1
    wanted = (
        tensor * 256 + ((r >> 3) & 7) * 32 + ((r >> 6) & 3) * 8 + (r >> 8) * 4 + (r & 3)
    )
    perm = jnp.where(c == wanted, 1.0, 0.0).astype(BF16)
    stack[...] = perm
    nt = (((1,), (1,)), ((), ()))

    loads[5].wait()
    pair = pl.ds(pl.multiple_of((z // 2) * 128, 128), 128)
    c0 = cot[0:128, pair].astype(F32)
    c1 = cot[128:256, pair].astype(F32)
    even = z % 2 == 0
    left = left_half((128, 128))
    cp[...] = jnp.where(
        left,
        jnp.where(even, c0, pltpu.roll(c0, 64, 1)),
        jnp.where(even, pltpu.roll(c1, 64, 1), c1),
    )
    for load in loads[6:]:
        load.wait()

    own.wait()
    pltpu.make_async_remote_copy(
        src_ref=src.at[pl.ds(0, NN - 1)], dst_ref=src.at[pl.ds(NN, NN - 1)],
        send_sem=a_send, recv_sem=a_recv, device_id=(z, node), device_id_type=MESH,
    ).wait_recv()
    for b in range(2):
        total = jnp.zeros((128, 256), F32)
        for k in range(0, 16, 2):
            weight = jnp.concatenate([tw[b, k], tw[b, k + 1]], axis=1)
            block = jnp.concatenate(
                [src[pl.ds(tsrc[b, k + e] * 8, 8)].reshape(128, 256) for e in range(2)], axis=0
            )
            total += jnp.dot(weight, block, preferred_element_type=F32)
        nm[pl.ds(b * 128, 128), :] = total.astype(BF16)

    def up(o, source):
        return pltpu.make_async_remote_copy(
            src_ref=rows_of(source, o), dst_ref=rows_of(rb.at[slot(o)], o),
            send_sem=b_send.at[sem(o)], recv_sem=b_recv.at[sem(o)],
            device_id=(zat(PARENT[o] - o), node), device_id_type=MESH,
        )

    ups = {o: up(o, pkb.at[zat(-o)]) for o in LEAVES}
    for pairs, leaves in (((4, 3, -3), (8, -8, 7, -7)), ((2, -2), (5, -5)), ((1, -1, 0), ())):
        for q in pairs:
            p = (z // 2 + q + 8) % 8
            cols = pl.ds(pl.multiple_of(p * 128, 128), 128)
            value = part[:, cols] + jnp.dot(nm[...], wn[:, cols], preferred_element_type=F32)
            p0, p1 = value[0:128], value[128:256]
            first = jnp.where(left, p0, pltpu.roll(p1, 64, 1))
            second = jnp.where(left, pltpu.roll(p0, 64, 1), p1)
            pk[2 * p] = first
            pk[2 * p + 1] = second
            pkb[2 * p] = first.astype(BF16)
            pkb[2 * p + 1] = second.astype(BF16)
        for o in leaves:
            ups[o].start()

    xpt[...] = (
        lax.dot_general(stack[:, 0:256], sf[...], nt, preferred_element_type=F32)
        + lax.dot_general(stack[:, 256:512], nm[...], nt, preferred_element_type=F32)
    ).astype(BF16)

    for o in (4, -4, 2, -2):
        ups[o].start()

    def summed(o, children):
        value = pk[zat(-o)]
        for child in children:
            ups[child].wait_recv()
            if child == 8:
                here, rest = value[0:64], value[64:128]
                here = here + rb[slot(8), 0:64].astype(F32)
                value = jnp.concatenate([here, rest], axis=0)
            elif child == -8:
                rest, here = value[0:64], value[64:128]
                here = here + rb[slot(8), 64:128].astype(F32)
                value = jnp.concatenate([rest, here], axis=0)
            else:
                value = value + rb[slot(child)].astype(F32)
        return value

    def hand_up(o, children):
        sb[slot(o)] = summed(o, children).astype(BF16)
        ups[o] = up(o, sb.at[slot(o)])
        ups[o].start()

    hand_up(6, (7, 8, 5))
    hand_up(-6, (-7, -8, -5))
    ups[1].start()
    ups[-1].start()
    hand_up(3, (4, 2, 6))
    hand_up(-3, (-4, -2, -6))
    pre = summed(0, (1, -1, 3, -3))

    s = jax.nn.sigmoid(pre)
    slope = s * (1.0 + pre * (1.0 - s))
    ag[0] = (cp[...] * slope).astype(BF16)

    def down(o):
        return pltpu.make_async_remote_copy(
            src_ref=rows_of(ag.at[slot(PARENT[o])], o), dst_ref=rows_of(ag.at[slot(o)], o),
            send_sem=c_send.at[sem(o)], recv_sem=c_recv.at[sem(o)],
            device_id=(zat(o - PARENT[o]), node), device_id_type=MESH,
        )

    downs = {}

    def forward(*offsets):
        for o in offsets:
            downs[o] = down(o)
            downs[o].start()

    def arrived(*offsets):
        for o in offsets:
            downs[o].wait_recv()

    forward(3, -3)
    value = pre * s
    value = value.T
    hid[:, 0:128] = value[0:64].astype(BF16)
    hid[:, 128:256] = value[64:128].astype(BF16)

    own_rows = pl.ds(pl.multiple_of(core * 256, 256), 256)
    other_rows = pl.ds(pl.multiple_of((1 - core) * 256, 256), 256)
    kept, copies = {}, {}

    def gathered(g):
        halves = []
        for q in (0, 2):
            a = ag[slot(GROUPS[g][q])].astype(F32)
            b = ag[slot(GROUPS[g][q + 1])].astype(F32)
            halves.append(jnp.concatenate(
                [
                    jnp.where(left, a, pltpu.roll(b, 64, 1)),
                    jnp.where(left, pltpu.roll(a, 64, 1), b),
                ], axis=0,
            ).astype(BF16))
        return jnp.concatenate(halves, axis=1)

    def terms(g):
        grad = gathered(g)
        cs[g] = jnp.dot(xpt[other_rows, :], grad, preferred_element_type=F32).astype(BF16)
        copies[g] = pltpu.make_async_remote_copy(
            src_ref=cs.at[g], dst_ref=cr.at[g], send_sem=dc_send.at[g], recv_sem=dc_recv.at[g],
            device_id=(z, node + 1 - 2 * core), device_id_type=MESH,
        )
        copies[g].start()
        kept[g] = jnp.dot(xpt[own_rows, :], grad, preferred_element_type=F32)

    def start_x(g):
        copies[g].wait_recv()
        total = kept[g] + cr[g].astype(F32)
        xs[g] = total
        xb[g] = total.astype(BF16)
        for i in (2, 1, 3):
            to = (x + i) % NX
            pltpu.make_async_remote_copy(
                src_ref=xb.at[g, pl.ds(pl.multiple_of(to * 64, 64), 64)], dst_ref=xr.at[g, i - 1],
                send_sem=dx_send.at[g], recv_sem=dx_recv.at[g],
                device_id=(z, (y * NX + to) * NC + core), device_id_type=MESH,
            ).start()

    def all_x(g):
        return pltpu.make_async_remote_copy(
            src_ref=xr.at[g], dst_ref=xr.at[g], send_sem=dx_send.at[g], recv_sem=dx_recv.at[g],
            device_id=(z, node), device_id_type=MESH,
        )

    def all_y(g):
        return pltpu.make_async_remote_copy(
            src_ref=yr.at[g], dst_ref=yr.at[g], send_sem=dy_send.at[g], recv_sem=dy_recv.at[g],
            device_id=(z, node), device_id_type=MESH,
        )

    def start_y(g):
        all_x(g).wait_recv()
        total = xs[g, pl.ds(pl.multiple_of(x * 64, 64), 64), :]
        for i in range(NX - 1):
            total = total + xr[g, i].astype(F32)
        total = total.reshape(NY, 8, 256)
        total = jnp.concatenate([total[:, :, 0:128], total[:, :, 128:256]], axis=1)
        ys[g] = total
        yb[g] = total.astype(BF16)
        for i in (4, 3, 5, 2, 6, 1, 7):
            to = (y + i) % NY
            pltpu.make_async_remote_copy(
                src_ref=yb.at[g, to], dst_ref=yr.at[g, i - 1],
                send_sem=dy_send.at[g], recv_sem=dy_recv.at[g],
                device_id=(z, (to * NX + x) * NC + core), device_id_type=MESH,
            ).start()

    half = lax.broadcasted_iota(jnp.int32, (8, 128), 1) // 64

    def finish(g):
        all_y(g).wait_recv()
        total = ys[g, y]
        for i in range(NY - 1):
            total = total + yr[g, i].astype(F32)
        for q in range(4):
            chunk = zat(-GROUPS[g][q])
            side = chunk % 2
            tile = total[(q // 2) * 8:(q // 2 + 1) * 8]
            tile = jnp.where(side == q % 2, tile, pltpu.roll(tile, 64, 1))
            fin[chunk // 2] = jnp.where(half == side, tile, fin[chunk // 2])

    fin[...] = jnp.zeros_like(fin)
    forward(1, -1)
    arrived(3)
    forward(6)
    arrived(-3)
    forward(-6)
    arrived(1, -1)
    terms(0)
    forward(4, 2, -4, -2)
    start_x(0)
    arrived(6)
    forward(8, 7, 5)
    arrived(-6)
    forward(-8, -7, -5)
    arrived(2, -2, 4)
    terms(1)
    arrived(-4, 5)
    terms(2)
    start_x(1)
    arrived(7, -5, -7, 8, -8)
    terms(3)
    start_x(2)
    start_y(0)
    start_x(3)
    start_y(1)
    start_y(2)
    start_y(3)
    finish(0)
    finish(1)
    finish(2)
    finish(3)
    for p in range(8):
        cols = pl.ds(p * 128, 128)
        grads[:, cols] = fin[p]

    pltpu.make_async_remote_copy(
        src_ref=out.at[pl.ds(0, NN - 1)], dst_ref=out.at[pl.ds(0, NN - 1)],
        send_sem=a_send, recv_sem=a_recv, device_id=(z, node), device_id_type=MESH,
    ).wait_send()
    for o in PARENT:
        ups[o].wait_send()
        downs[o].wait_send()
    for g in range(4):
        copies[g].wait_send()
        all_x(g).wait_send()
        all_y(g).wait_send()


def write_out(hidden, grads, hid, grad_self, grad_neigh, sems):
    copies = [
        pltpu.make_async_copy(hidden, hid, sems.at[0]),
        pltpu.make_async_copy(grads.at[0:4], grad_self, sems.at[1]),
        pltpu.make_async_copy(grads.at[4:8], grad_neigh, sems.at[2]),
    ]
    for copy in copies:
        copy.start()
    for copy in copies:
        copy.wait()


def on_device(
    features, seed_ids, send_rows, send_counts, tile_src, tile_weights, w_self, w_neigh, cotangent
):
    hbm = pl.BlockSpec(memory_space=pltpu.HBM)
    vmem = pl.BlockSpec(memory_space=pltpu.VMEM)
    dma = pltpu.SemaphoreType.DMA
    hidden_t, grads = pl.pallas_call(
        kernel,
        out_shape=(
            jax.ShapeDtypeStruct((64, 256), BF16),
            jax.ShapeDtypeStruct((8, 1024), F32),
        ),
        in_specs=[hbm] * 9,
        out_specs=(vmem, vmem),
        scratch_shapes=[
            pltpu.VMEM((16, 64), jnp.int32),
            pltpu.VMEM((1, 64), jnp.int32),
            pltpu.VMEM((2, 128), jnp.int32),
            pltpu.SMEM((2, 16), jnp.int32),
            pltpu.VMEM((128, 128), F32),
            pltpu.VMEM((2 * NN, 16, 256), BF16),
            pltpu.VMEM((NN, 16, 256), BF16),
            pltpu.VMEM((2, 16, 128, 128), BF16),
            pltpu.VMEM((256, 1024), BF16),
            pltpu.VMEM((256, 1024), BF16),
            pltpu.VMEM((256, 1024), BF16),
            pltpu.VMEM((256, 256), BF16),
            pltpu.VMEM((256, 256), BF16),
            pltpu.VMEM((256, 1024), F32),
            pltpu.VMEM((NZ, 128, 128), F32),
            pltpu.VMEM((NZ, 128, 128), BF16),
            pltpu.VMEM((NZ, 128, 128), BF16),
            pltpu.VMEM((NZ, 128, 128), BF16),
            pltpu.VMEM((128, 128), F32),
            pltpu.VMEM((NZ, 128, 128), BF16),
            pltpu.VMEM((512, 256), BF16),
            pltpu.VMEM((512, 512), BF16),
            pltpu.VMEM((4, 256, 256), BF16),
            pltpu.VMEM((4, 256, 256), BF16),
            pltpu.VMEM((4, 256, 256), F32),
            pltpu.VMEM((4, 256, 256), BF16),
            pltpu.VMEM((4, NX - 1, 64, 256), BF16),
            pltpu.VMEM((4, NY, 16, 128), F32),
            pltpu.VMEM((4, NY, 16, 128), BF16),
            pltpu.VMEM((4, NY - 1, 16, 128), BF16),
            pltpu.VMEM((8, 8, 128), F32),
            dma((10,)),
            dma,
            dma,
            dma((NZ,)),
            dma((NZ,)),
            dma((NZ,)),
            dma((NZ,)),
            dma((4,)),
            dma((4,)),
            dma((4,)),
            dma((4,)),
            dma((4,)),
            dma((4,)),
        ],
        compiler_params=pltpu.CompilerParams(
            collective_id=0, has_side_effects=True, vmem_limit_bytes=60 * 1024 * 1024
        ),
        name="sage_layer",
    )(
        features.reshape(64, 16, 256), send_rows[0].T, send_counts, seed_ids.reshape(2, 128),
        tile_src, tile_weights, w_self, w_neigh, cotangent,
    )
    hidden_t, grad_self, grad_neigh = pl.pallas_call(
        write_out,
        out_shape=(
            jax.ShapeDtypeStruct((64, 256), BF16),
            jax.ShapeDtypeStruct((4, 1024), F32),
            jax.ShapeDtypeStruct((4, 1024), F32),
        ),
        in_specs=[vmem] * 2,
        out_specs=(hbm,) * 3,
        scratch_shapes=[dma((3,))],
        name="write_out",
    )(hidden_t, grads)
    return hidden_t.T, grad_self, grad_neigh


def solution(mesh):
    in_specs = (
        P("node", "col"),
        P("node"),
        P("node", None, None),
        P("node", None),
        P("node", None),
        P("node", None, None, None),
        P("col", None),
        P("col", None),
        P("node", None),
    )
    out_specs = (P("node", "col"), P(("col", "node"), None), P(("col", "node"), None))
    return jax.shard_map(
        on_device, mesh=mesh, in_specs=in_specs, out_specs=out_specs, check_vma=False
    )
```

```python
import jax
import jax.numpy as jnp
from jax import lax
from jax.experimental import pallas as pl
from jax.experimental.pallas import tpu as pltpu
from jax.sharding import PartitionSpec as P

MESH = pl.DeviceIdType.MESH
F32 = jnp.float32
BF16 = jnp.bfloat16

NZ, NY, NX, NC = 16, 8, 4, 2
NN = NY * NX * NC
NBAR = NN - 1 + 8

PARENT = {
    8: 6, -8: -6, 7: 6, 5: 6, -7: -6, -5: -6, 6: 3, -6: -3,
    4: 3, 2: 3, -4: -3, -2: -3, 3: 0, -3: 0, 1: 0, -1: 0,
}
UP = {**PARENT, 6: 0, -6: 0}
LEAVES = (8, -8, 7, -7, 5, -5, 4, -4, 2, -2, 1, -1)
HALVES = {8: 0, -8: 64}
GROUPS = ((0, 1, -1, 3), (-3, 2, -2, 4), (-4, 6, -6, 5), (7, -5, -7, 8))


def slot(offset):
    return offset % NZ


def sem(offset):
    return 0 if offset == -8 else slot(offset)


def rows_of(ref, offset):
    return ref.at[pl.ds(HALVES[offset], 64)] if offset in HALVES else ref


def left_half(shape):
    return lax.broadcasted_iota(jnp.int32, shape, 1) < 64


def one_hot_rows(spread):
    lane = lax.broadcasted_iota(jnp.int32, (128, 128), 1).astype(F32)
    parts = [
        jnp.where(spread == lane + 128.0 * j, 1.0, 0.0).astype(BF16) for j in range(8)
    ]
    return jnp.concatenate(parts, axis=1)


def kernel(
    feat, rows_hbm, counts_hbm, seed_hbm, tsrc_hbm, tw_hbm, ws_hbm, wn_hbm, cot_hbm,
    hid, grads,
    rows, counts, seed, tsrc, slots, wc, mean, src, out, tw, ws, wn, cot, sf, nm, part, pk, pkb, rb, sb, cp, ag, xpt, stack,
    cs, cr, xs, xb, xr, ys, yb, yr, fin,
    lsem, a_send, a_recv, b_send, b_recv, c_send, c_recv,
    dc_send, dc_recv, dx_send, dx_recv, dy_send, dy_recv,
):
    z = lax.axis_index("col")
    node = lax.axis_index("node")
    core = node % NC
    x = (node // NC) % NX
    y = node // (NC * NX)

    def zat(offset):
        return (z + offset + NZ) % NZ

    loads = [
        pltpu.make_async_copy(a, b, lsem.at[i])
        for i, (a, b) in enumerate((
            (rows_hbm, rows), (counts_hbm, counts), (feat, src.at[pl.ds(0, NN)]), (seed_hbm, seed),
            (ws_hbm, ws), (cot_hbm, cot), (tsrc_hbm, tsrc), (tw_hbm, tw), (wn_hbm, wn),
        ))
    ]
    for load in loads[:3]:
        load.start()

    barrier = pltpu.get_barrier_semaphore()
    for d in (4, 3, 5, 2, 6, 1, 7, 0):
        for j in range(8):
            if d or j:
                to = ((y + d) % NY) * 8 + (node + j) % 8
                pl.semaphore_signal(barrier, inc=1, device_id=(z, to), device_id_type=MESH)
    for d in (6, -6, 3, -3, 2, -2, 1, -1):
        pl.semaphore_signal(barrier, inc=1, device_id=(zat(d), node), device_id_type=MESH)
    for load in loads[3:]:
        load.start()

    loads[0].wait()
    loads[1].wait()
    live = lax.broadcasted_iota(jnp.int32, (16, 64), 0) < counts[...]
    table = jnp.where(live, rows[...], -1).astype(F32)
    table = jnp.concatenate([table, jnp.zeros((16, 64), F32)], axis=1)
    slots[...] = jnp.concatenate([table, jnp.zeros((112, 128), F32)], axis=0).T
    loads[2].wait()
    feats = src[pl.ds(0, NN)].reshape(1024, 256)
    own_slot = (
        lax.broadcasted_iota(jnp.int32, (128, 128), 0) % 16
        == lax.broadcasted_iota(jnp.int32, (128, 128), 1)
    )

    def gather(yy):
        tile = slots[pl.ds(pl.multiple_of(yy * 8, 8), 8), :]
        tile = jnp.broadcast_to(tile[:, None, :], (8, 16, 128)).reshape(128, 128)
        spread = jnp.sum(jnp.where(own_slot, tile, 0.0), axis=1, keepdims=True)
        hot = one_hot_rows(spread)
        picked = jnp.dot(hot, feats, preferred_element_type=F32).astype(BF16)
        out[pl.ds(pl.multiple_of(yy * 8, 8), 8)] = picked.reshape(8, 16, 256)

    def send_rows(to):
        pltpu.make_async_remote_copy(
            src_ref=out.at[to], dst_ref=src.at[NN + node], send_sem=a_send, recv_sem=a_recv,
            device_id=(z, to), device_id_type=MESH,
        ).start()

    for step, d in enumerate((4, 3, 5, 2, 6, 1, 7)):
        yy = (y + d) % NY
        gather(yy)
        if step == 0:
            pl.semaphore_wait(barrier, NBAR)
        for j in range(8):
            send_rows(yy * 8 + (node + j) % 8)
    gather(y)
    for j in range(1, 8):
        send_rows(y * 8 + (node + j) % 8)
    own = pltpu.make_async_copy(out.at[node], src.at[NN + node], lsem.at[9])
    own.start()

    loads[3].wait()
    for b in range(2):
        hot = one_hot_rows(jnp.broadcast_to(seed[b:b + 1, :].astype(F32), (128, 128)).T)
        sf[pl.ds(b * 128, 128), :] = jnp.dot(hot, feats, preferred_element_type=F32).astype(BF16)
    loads[4].wait()
    part[...] = jnp.dot(sf[...], ws[...], preferred_element_type=F32)

    r = lax.broadcasted_iota(jnp.int32, (512, 512), 0)
    c = lax.broadcasted_iota(jnp.int32, (512, 512), 1)
    tensor = (r >> 2) & 1
    wanted = (
        tensor * 256 + ((r >> 3) & 7) * 32 + ((r >> 6) & 3) * 8 + (r >> 8) * 4 + (r & 3)
    )
    perm = jnp.where(c == wanted, 1.0, 0.0).astype(BF16)
    stack[...] = perm
    nt = (((1,), (1,)), ((), ()))

    loads[5].wait()
    pair = pl.ds(pl.multiple_of((z // 2) * 128, 128), 128)
    c0 = cot[0:128, pair].astype(F32)
    c1 = cot[128:256, pair].astype(F32)
    even = z % 2 == 0
    left = left_half((128, 128))
    cp[...] = jnp.where(
        left,
        jnp.where(even, c0, pltpu.roll(c0, 64, 1)),
        jnp.where(even, pltpu.roll(c1, 64, 1), c1),
    )
    for load in loads[6:]:
        load.wait()

    def by_source(t, carry):
        cols = pl.ds(pl.multiple_of((t % 2) * 128, 128), 128)
        for b in range(2):
            total = jnp.zeros((128, 128), F32)
            for k in range(16):
                total += jnp.where(tsrc[b, k] == t, tw[b, k].astype(F32), 0.0)
            high = total.astype(BF16)
            wc[t // 2, pl.ds(b * 128, 128), cols] = high
            wc[t // 2, pl.ds(256 + b * 128, 128), cols] = (total - high.astype(F32)).astype(BF16)
        return carry

    lax.fori_loop(0, 16, by_source, 0)

    def blocks_times(pairs):
        total = jnp.zeros((512, 256), F32)
        for pair_of in pairs:
            block = src[pl.ds(pair_of * 16, 16)].reshape(256, 256)
            total += jnp.dot(wc[pair_of], block, preferred_element_type=F32)
        return total[0:256] + total[256:512]

    mean[...] = blocks_times(range(4))

    own.wait()
    pltpu.make_async_remote_copy(
        src_ref=src.at[pl.ds(0, NN - 1)], dst_ref=src.at[pl.ds(NN, NN - 1)],
        send_sem=a_send, recv_sem=a_recv, device_id=(z, node), device_id_type=MESH,
    ).wait_recv()
    nm[...] = (mean[...] + blocks_times(range(4, 8))).astype(BF16)

    def up(o, source):
        return pltpu.make_async_remote_copy(
            src_ref=rows_of(source, o), dst_ref=rows_of(rb.at[slot(o)], o),
            send_sem=b_send.at[sem(o)], recv_sem=b_recv.at[sem(o)],
            device_id=(zat(UP[o] - o), node), device_id_type=MESH,
        )

    ups = {o: up(o, pkb.at[zat(-o)]) for o in LEAVES}
    for pairs, leaves in (((4, 3, -3), (8, -8, 7, -7)), ((2, -2), (5, -5)), ((1, -1, 0), ())):
        for q in pairs:
            p = (z // 2 + q + 8) % 8
            cols = pl.ds(pl.multiple_of(p * 128, 128), 128)
            value = part[:, cols] + jnp.dot(nm[...], wn[:, cols], preferred_element_type=F32)
            p0, p1 = value[0:128], value[128:256]
            first = jnp.where(left, p0, pltpu.roll(p1, 64, 1))
            second = jnp.where(left, pltpu.roll(p0, 64, 1), p1)
            pk[2 * p] = first
            pk[2 * p + 1] = second
            pkb[2 * p] = first.astype(BF16)
            pkb[2 * p + 1] = second.astype(BF16)
        for o in leaves:
            ups[o].start()

    xpt[...] = (
        lax.dot_general(stack[:, 0:256], sf[...], nt, preferred_element_type=F32)
        + lax.dot_general(stack[:, 256:512], nm[...], nt, preferred_element_type=F32)
    ).astype(BF16)

    for o in (4, -4, 2, -2):
        ups[o].start()

    def summed(o, children):
        value = pk[zat(-o)]
        for child in children:
            ups[child].wait_recv()
            if child == 8:
                here, rest = value[0:64], value[64:128]
                here = here + rb[slot(8), 0:64].astype(F32)
                value = jnp.concatenate([here, rest], axis=0)
            elif child == -8:
                rest, here = value[0:64], value[64:128]
                here = here + rb[slot(8), 64:128].astype(F32)
                value = jnp.concatenate([rest, here], axis=0)
            else:
                value = value + rb[slot(child)].astype(F32)
        return value

    def hand_up(o, children):
        sb[slot(o)] = summed(o, children).astype(BF16)
        ups[o] = up(o, sb.at[slot(o)])
        ups[o].start()

    hand_up(6, (7, 8, 5))
    hand_up(-6, (-7, -8, -5))
    ups[1].start()
    ups[-1].start()
    hand_up(3, (4, 2))
    hand_up(-3, (-4, -2))
    pre = summed(0, (1, -1, 3, -3, 6, -6))

    s = jax.nn.sigmoid(pre)
    slope = s * (1.0 + pre * (1.0 - s))
    ag[0] = (cp[...] * slope).astype(BF16)

    def down(o):
        return pltpu.make_async_remote_copy(
            src_ref=rows_of(ag.at[slot(PARENT[o])], o), dst_ref=rows_of(ag.at[slot(o)], o),
            send_sem=c_send.at[sem(o)], recv_sem=c_recv.at[sem(o)],
            device_id=(zat(o - PARENT[o]), node), device_id_type=MESH,
        )

    downs = {}

    def forward(*offsets):
        for o in offsets:
            downs[o] = down(o)
            downs[o].start()

    def arrived(*offsets):
        for o in offsets:
            downs[o].wait_recv()

    forward(3, -3)
    value = pre * s
    value = value.T
    hid[:, 0:128] = value[0:64].astype(BF16)
    hid[:, 128:256] = value[64:128].astype(BF16)

    own_rows = pl.ds(pl.multiple_of(core * 256, 256), 256)
    other_rows = pl.ds(pl.multiple_of((1 - core) * 256, 256), 256)
    kept, copies = {}, {}

    def gathered(g):
        halves = []
        for q in (0, 2):
            a = ag[slot(GROUPS[g][q])].astype(F32)
            b = ag[slot(GROUPS[g][q + 1])].astype(F32)
            halves.append(jnp.concatenate(
                [
                    jnp.where(left, a, pltpu.roll(b, 64, 1)),
                    jnp.where(left, pltpu.roll(a, 64, 1), b),
                ], axis=0,
            ).astype(BF16))
        return jnp.concatenate(halves, axis=1)

    def terms(g):
        grad = gathered(g)
        cs[g] = jnp.dot(xpt[other_rows, :], grad, preferred_element_type=F32).astype(BF16)
        copies[g] = pltpu.make_async_remote_copy(
            src_ref=cs.at[g], dst_ref=cr.at[g], send_sem=dc_send.at[g], recv_sem=dc_recv.at[g],
            device_id=(z, node + 1 - 2 * core), device_id_type=MESH,
        )
        copies[g].start()
        kept[g] = jnp.dot(xpt[own_rows, :], grad, preferred_element_type=F32)

    def start_x(g):
        copies[g].wait_recv()
        total = kept[g] + cr[g].astype(F32)
        xs[g] = total
        xb[g] = total.astype(BF16)
        for i in (2, 1, 3):
            to = (x + i) % NX
            pltpu.make_async_remote_copy(
                src_ref=xb.at[g, pl.ds(pl.multiple_of(to * 64, 64), 64)], dst_ref=xr.at[g, i - 1],
                send_sem=dx_send.at[g], recv_sem=dx_recv.at[g],
                device_id=(z, (y * NX + to) * NC + core), device_id_type=MESH,
            ).start()

    def all_x(g):
        return pltpu.make_async_remote_copy(
            src_ref=xr.at[g], dst_ref=xr.at[g], send_sem=dx_send.at[g], recv_sem=dx_recv.at[g],
            device_id=(z, node), device_id_type=MESH,
        )

    def all_y(g):
        return pltpu.make_async_remote_copy(
            src_ref=yr.at[g], dst_ref=yr.at[g], send_sem=dy_send.at[g], recv_sem=dy_recv.at[g],
            device_id=(z, node), device_id_type=MESH,
        )

    def start_y(g):
        all_x(g).wait_recv()
        total = xs[g, pl.ds(pl.multiple_of(x * 64, 64), 64), :]
        for i in range(NX - 1):
            total = total + xr[g, i].astype(F32)
        total = total.reshape(NY, 8, 256)
        total = jnp.concatenate([total[:, :, 0:128], total[:, :, 128:256]], axis=1)
        ys[g] = total
        yb[g] = total.astype(BF16)
        for i in (4, 3, 5, 2, 6, 1, 7):
            to = (y + i) % NY
            pltpu.make_async_remote_copy(
                src_ref=yb.at[g, to], dst_ref=yr.at[g, i - 1],
                send_sem=dy_send.at[g], recv_sem=dy_recv.at[g],
                device_id=(z, (to * NX + x) * NC + core), device_id_type=MESH,
            ).start()

    half = lax.broadcasted_iota(jnp.int32, (8, 128), 1) // 64

    def finish(g):
        all_y(g).wait_recv()
        total = ys[g, y]
        for i in range(NY - 1):
            total = total + yr[g, i].astype(F32)
        for q in range(4):
            chunk = zat(-GROUPS[g][q])
            side = chunk % 2
            tile = total[(q // 2) * 8:(q // 2 + 1) * 8]
            tile = jnp.where(side == q % 2, tile, pltpu.roll(tile, 64, 1))
            fin[chunk // 2] = jnp.where(half == side, tile, fin[chunk // 2])

    fin[...] = jnp.zeros_like(fin)
    forward(1, -1)
    arrived(3)
    forward(6)
    arrived(-3)
    forward(-6)
    arrived(1, -1)
    terms(0)
    forward(4, 2, -4, -2)
    start_x(0)
    arrived(6)
    forward(8, 7, 5)
    arrived(-6)
    forward(-8, -7, -5)
    arrived(2, -2, 4)
    terms(1)
    arrived(-4, 5)
    terms(2)
    start_x(1)
    arrived(7, -5, -7, 8, -8)
    terms(3)
    start_x(2)
    start_y(0)
    start_x(3)
    start_y(1)
    start_y(2)
    start_y(3)
    finish(0)
    finish(1)
    finish(2)
    finish(3)
    for p in range(8):
        cols = pl.ds(p * 128, 128)
        grads[:, cols] = fin[p]

    pltpu.make_async_remote_copy(
        src_ref=out.at[pl.ds(0, NN - 1)], dst_ref=out.at[pl.ds(0, NN - 1)],
        send_sem=a_send, recv_sem=a_recv, device_id=(z, node), device_id_type=MESH,
    ).wait_send()
    for o in PARENT:
        ups[o].wait_send()
        downs[o].wait_send()
    for g in range(4):
        copies[g].wait_send()
        all_x(g).wait_send()
        all_y(g).wait_send()


def write_out(hidden, grads, hid, grad_self, grad_neigh, sems):
    copies = [
        pltpu.make_async_copy(hidden, hid, sems.at[0]),
        pltpu.make_async_copy(grads.at[0:4], grad_self, sems.at[1]),
        pltpu.make_async_copy(grads.at[4:8], grad_neigh, sems.at[2]),
    ]
    for copy in copies:
        copy.start()
    for copy in copies:
        copy.wait()


def on_device(
    features, seed_ids, send_rows, send_counts, tile_src, tile_weights, w_self, w_neigh, cotangent
):
    hbm = pl.BlockSpec(memory_space=pltpu.HBM)
    vmem = pl.BlockSpec(memory_space=pltpu.VMEM)
    dma = pltpu.SemaphoreType.DMA
    hidden_t, grads = pl.pallas_call(
        kernel,
        out_shape=(
            jax.ShapeDtypeStruct((64, 256), BF16),
            jax.ShapeDtypeStruct((8, 1024), F32),
        ),
        in_specs=[hbm] * 9,
        out_specs=(vmem, vmem),
        scratch_shapes=[
            pltpu.VMEM((16, 64), jnp.int32),
            pltpu.VMEM((1, 64), jnp.int32),
            pltpu.VMEM((2, 128), jnp.int32),
            pltpu.SMEM((2, 16), jnp.int32),
            pltpu.VMEM((128, 128), F32),
            pltpu.VMEM((8, 512, 256), BF16),
            pltpu.VMEM((256, 256), F32),
            pltpu.VMEM((2 * NN, 16, 256), BF16),
            pltpu.VMEM((NN, 16, 256), BF16),
            pltpu.VMEM((2, 16, 128, 128), BF16),
            pltpu.VMEM((256, 1024), BF16),
            pltpu.VMEM((256, 1024), BF16),
            pltpu.VMEM((256, 1024), BF16),
            pltpu.VMEM((256, 256), BF16),
            pltpu.VMEM((256, 256), BF16),
            pltpu.VMEM((256, 1024), F32),
            pltpu.VMEM((NZ, 128, 128), F32),
            pltpu.VMEM((NZ, 128, 128), BF16),
            pltpu.VMEM((NZ, 128, 128), BF16),
            pltpu.VMEM((NZ, 128, 128), BF16),
            pltpu.VMEM((128, 128), F32),
            pltpu.VMEM((NZ, 128, 128), BF16),
            pltpu.VMEM((512, 256), BF16),
            pltpu.VMEM((512, 512), BF16),
            pltpu.VMEM((4, 256, 256), BF16),
            pltpu.VMEM((4, 256, 256), BF16),
            pltpu.VMEM((4, 256, 256), F32),
            pltpu.VMEM((4, 256, 256), BF16),
            pltpu.VMEM((4, NX - 1, 64, 256), BF16),
            pltpu.VMEM((4, NY, 16, 128), F32),
            pltpu.VMEM((4, NY, 16, 128), BF16),
            pltpu.VMEM((4, NY - 1, 16, 128), BF16),
            pltpu.VMEM((8, 8, 128), F32),
            dma((10,)),
            dma,
            dma,
            dma((NZ,)),
            dma((NZ,)),
            dma((NZ,)),
            dma((NZ,)),
            dma((4,)),
            dma((4,)),
            dma((4,)),
            dma((4,)),
            dma((4,)),
            dma((4,)),
        ],
        compiler_params=pltpu.CompilerParams(
            collective_id=0, has_side_effects=True, vmem_limit_bytes=60 * 1024 * 1024
        ),
        name="sage_layer",
    )(
        features.reshape(64, 16, 256), send_rows[0].T, send_counts, seed_ids.reshape(2, 128),
        tile_src, tile_weights, w_self, w_neigh, cotangent,
    )
    hidden_t, grad_self, grad_neigh = pl.pallas_call(
        write_out,
        out_shape=(
            jax.ShapeDtypeStruct((64, 256), BF16),
            jax.ShapeDtypeStruct((4, 1024), F32),
            jax.ShapeDtypeStruct((4, 1024), F32),
        ),
        in_specs=[vmem] * 2,
        out_specs=(hbm,) * 3,
        scratch_shapes=[dma((3,))],
        name="write_out",
    )(hidden_t, grads)
    return hidden_t.T, grad_self, grad_neigh


def solution(mesh):
    in_specs = (
        P("node", "col"),
        P("node"),
        P("node", None, None),
        P("node", None),
        P("node", None),
        P("node", None, None, None),
        P("col", None),
        P("col", None),
        P("node", None),
    )
    out_specs = (P("node", "col"), P(("col", "node"), None), P(("col", "node"), None))
    return jax.shard_map(
        on_device, mesh=mesh, in_specs=in_specs, out_specs=out_specs, check_vma=False
    )
```
